32 devices in a mesh: groups: 2 (over x), ctx: 16 (over z, y, core).
Axes of the slice: x: 2, y: 2, z: 4, core: 2. Of those that a mesh axis runs over, the one named last changes fastest.
Arguments:
- pool_keys: bfloat16 [4096, 1024], P(('groups', 'ctx')), parts along dimension 0, may hold values from -6 to 6
- pool_values: bfloat16 [4096, 1024], P(('groups', 'ctx')), parts along dimension 0, may hold values from -6 to 6
- key_scales: float32 [256, 8], P(('groups', 'ctx')), parts along dimension 0, may hold values from 0.25 to 2
- value_scales: float32 [256, 8], P(('groups', 'ctx')), parts along dimension 0, may hold values from 0.25 to 2
- page_source: int32 [256], P('groups'), parts along dimension 0, may hold values from 0 to 127, as said below
- page_lengths: int32 [256], P('groups'), parts along dimension 0, may hold values from 10 to 16
- page_offsets: int32 [256], P('groups'), parts along dimension 0, may hold values from 0 to 1899, as said below
- query_positions: int32 [256], P('groups'), parts along dimension 0, may hold values from 0 to 2047
- queries: bfloat16 [256, 16384], P('groups', 'ctx'), parts along dimension 0, may hold values from -64 to 64
- out_weight: bfloat16 [16384, 16384], P('ctx'), may hold values from -0.046875 to 0.046875
Outputs:
- new_keys: bfloat16 [4096, 1024], P(('groups', 'ctx')), parts along dimension 0
- new_values: bfloat16 [4096, 1024], P(('groups', 'ctx')), parts along dimension 0
- output: bfloat16 [256, 16384], P('groups', 'ctx'), parts along dimension 0
The draws below stay inside these ranges and needn't reach their ends.
There are 2 independent parts, one for each index of `groups`. The reference program is written for one: setup_inputs(seed, part) draws one part's arguments, and reference() takes and returns one part's arrays. A program takes and returns all parts, laid end to end along the dimension named above; an argument that names none is the same for every part. Nothing has to cross between parts.
Inputs may be any that keep to these rules, and one draw needn't show every extreme that they name: `page_source`: a permutation of the pool pages; the 8 pages of one device's part of the new context come from 8 different devices, and the 8 pool pages of one device go to 8 different devices. page_offsets[0] is 0, and page_offsets[c + 1] - page_offsets[c] is page_lengths[c] plus 0 to 4.
All inputs are finite; a program needn't handle non-finite values.
Results may differ from the reference program's by a relative error of at most 0.012.
The reference program's roundings to bfloat16 on the way count: a program that leaves them out, or rounds other values in their place, can miss the bound.
Values may be sent and summed in bfloat16 or wider, within the bound.
A program may use at most 128 MiB of HBM per device.

```python
import math
import jax
import jax.numpy as jnp
from jax import lax

D = 16384
H = 128
KV = 8
HD = 128
PAGE = 16
QN = 128
SLOTS = 8
NPAGES = 128


def draw_page_source(key, part):
    owners = NPAGES // SLOTS
    key_parts = jax.random.split(jax.random.fold_in(key, 11), 4)
    shifts = jax.random.permutation(key_parts[0], owners)[:SLOTS]
    relabel = jax.random.permutation(key_parts[1], owners)
    local_slot = jax.vmap(lambda item: jax.random.permutation(item, SLOTS))(jax.random.split(key_parts[2], owners))
    arrival_order = jax.vmap(lambda item: jax.random.permutation(item, SLOTS))(jax.random.split(key_parts[3], owners))
    sources = jnp.arange(owners)[:, None]
    which = jnp.arange(SLOTS)[None, :]
    owner_device = relabel[(sources + shifts[None, :]) % owners]
    position = owner_device * SLOTS + arrival_order[owner_device, which]
    source_slot = sources * SLOTS + local_slot
    source_table = jnp.zeros((NPAGES,), jnp.int32).at[position.reshape(-1)].set(source_slot.reshape(-1).astype(jnp.int32))
    return source_table.astype(jnp.int32)


def page_layout(key):
    key_parts = jax.random.split(jax.random.fold_in(key, 23), 4)
    head_count = NPAGES - 1
    length_spread = 3 * PAGE // 8 + 1
    gap_spread = PAGE // 4 + 1
    counter = jnp.arange(head_count, dtype=jnp.int32)
    head_lengths = jax.random.permutation(key_parts[0], PAGE - 3 * PAGE // 8 + counter % length_spread)
    head_gaps = jax.random.permutation(key_parts[1], counter % gap_spread)
    last_length = jax.random.randint(key_parts[2], (1,), PAGE - 3 * PAGE // 8, PAGE + 1)
    last_gap = jax.random.randint(key_parts[3], (1,), 0, PAGE // 4 + 1)
    lengths = jnp.concatenate([head_lengths, last_length]).astype(jnp.int32)
    page_gaps = jnp.concatenate([head_gaps, last_gap]).astype(jnp.int32)
    steps_total = lengths + page_gaps
    offsets = jnp.cumsum(steps_total) - steps_total
    return (lengths.astype(jnp.int32), offsets.astype(jnp.int32))


def draw_page_lengths(key, part):
    return page_layout(key)[0]


def draw_page_offsets(key, part):
    return page_layout(key)[1]


def draw_queries(key, part):
    first_key, second_key = jax.random.split(jax.random.fold_in(key, 31))
    normal_part = jnp.clip(jax.random.normal(first_key, (QN, H * HD), jnp.float32), -4.0, 4.0)
    scales = jnp.exp(jax.random.uniform(second_key, (QN, 1), jnp.float32, 0.0, math.log(2.0)))
    return (normal_part * scales).astype(jnp.bfloat16)


def set_ends(drawn, key, low, largest):
    longest = drawn.shape.index(max(drawn.shape))
    spots = []
    for shift in (0, 1):
        where = [jax.random.randint(jax.random.fold_in(key, axis), (), 0, length) for axis, length in enumerate(drawn.shape)]
        where[longest] = (where[longest] + shift) % drawn.shape[longest]
        spots.append(tuple(where))
    return drawn.at[spots[0]].set(low).at[spots[1]].set(largest)


def shard_levels(stream_key, extent, pieces, low, high):
    level, own = 1.0, jax.random.fold_in(stream_key, 6)
    for axis_at, parts in pieces:
        steps = jnp.exp(jax.random.uniform(jax.random.fold_in(own, axis_at), (parts,), jnp.float32, low / len(pieces), high / len(pieces)))
        level = level * jnp.repeat(steps, extent[axis_at] // parts).reshape([-1 if axis == axis_at else 1 for axis in range(len(extent))])
    return level


def scatter_about(rng, dims, width, bound, shards=(), kind=jnp.bfloat16):
    array = width * jax.random.normal(rng, dims, jnp.float32)
    if shards:
        array = array * shard_levels(rng, dims, shards, -0.22, 0.18)
    return jnp.clip(array, -bound, bound).astype(kind)


def setup_inputs(seed: int = 0, part: int = 0) -> dict:
    splits = jax.random.split(jax.random.key(seed), 11)
    part_splits = jax.random.split(jax.random.fold_in(splits[10], part), 11)
    return {
        "pool_keys": scatter_about(part_splits[0], (NPAGES * PAGE, KV * HD), 1.0, 6.0, ((0, 16),)),
        "pool_values": scatter_about(part_splits[1], (NPAGES * PAGE, KV * HD), 1.0, 6.0, ((0, 16),)),
        "key_scales": jnp.clip(jnp.exp(math.log(2.0) - 2.0794415 * jax.random.uniform(part_splits[2], (NPAGES, KV), jnp.float32) ** shard_levels(part_splits[2], (NPAGES, KV), ((0, 16),), -0.2, 0.2)), 0.25, 2.0),
        "value_scales": jnp.clip(jnp.exp(math.log(2.0) - 2.0794415 * jax.random.uniform(part_splits[3], (NPAGES, KV), jnp.float32) ** shard_levels(part_splits[3], (NPAGES, KV), ((0, 16),), -0.2, 0.2)), 0.25, 2.0),
        "page_source": draw_page_source(jax.random.fold_in(jax.random.fold_in(splits[10], part), 71), part),
        "page_lengths": draw_page_lengths(jax.random.fold_in(jax.random.fold_in(splits[10], part), 71), part),
        "page_offsets": draw_page_offsets(jax.random.fold_in(jax.random.fold_in(splits[10], part), 71), part),
        "query_positions": set_ends(jax.random.randint(part_splits[7], (QN,), 0, NPAGES * PAGE), jax.random.fold_in(part_splits[7], 1), 0, (NPAGES * PAGE) - 1).astype(jnp.int32),
        "queries": draw_queries(jax.random.fold_in(jax.random.fold_in(splits[10], part), 71), part),
        "out_weight": scatter_about(splits[9], (H * HD, D), (H * HD) ** -0.5, 0.046875, ((0, 16),)),
    }


rope_theta = 500000.0
scale_factor = 8.0
low_factor = 1.0
high_factor = 4.0
old_context = 8192.0
masked_score = -1.0e30


def inverse_freq():
    exponent = jnp.arange(0, HD, 2).astype(jnp.float32) / HD
    base_freq = 1.0 / (rope_theta ** exponent)
    wavelength = 2.0 * math.pi / base_freq
    smooth = (old_context / wavelength - low_factor) / (high_factor - low_factor)
    blended = (1.0 - smooth) * base_freq / scale_factor + smooth * base_freq
    short_wave = wavelength < old_context / high_factor
    longer = wavelength > old_context / low_factor
    return jnp.where(short_wave, base_freq, jnp.where(longer, base_freq / scale_factor, blended))


def rotate(values, positions):
    angle = positions.astype(jnp.float32)[:, None] * inverse_freq()[None, :]
    cosine = jnp.cos(angle)[:, None, :]
    sine_part = jnp.sin(angle)[:, None, :]
    half_size = values.shape[-1] // 2
    first_half = values[..., :half_size]
    second = values[..., half_size:]
    return jnp.concatenate([first_half * cosine - second * sine_part, second * cosine + first_half * sine_part], axis=-1)


def reference(pool_keys, pool_values, key_scales, value_scales, page_source, page_lengths, page_offsets, query_positions, queries, out_weight):
    in_page = jnp.arange(PAGE, dtype=jnp.int32)
    live_mask = in_page[None, :] < page_lengths[:, None]
    live_float = live_mask.reshape(-1).astype(jnp.float32)[:, None, None]
    slot_keys = pool_keys.reshape(NPAGES, PAGE, KV, HD).astype(jnp.float32) * key_scales[:, None, :, None]
    slot_values = pool_values.reshape(NPAGES, PAGE, KV, HD).astype(jnp.float32) * value_scales[:, None, :, None]
    moved_keys = slot_keys[page_source].reshape(NPAGES * PAGE, KV, HD)
    moved_values = slot_values[page_source].reshape(NPAGES * PAGE, KV, HD)
    page_shift = jnp.repeat(page_offsets, PAGE)
    turned = rotate(moved_keys, page_shift)
    new_keys = lax.optimization_barrier((turned * live_float).astype(jnp.bfloat16))
    new_values = lax.optimization_barrier((moved_values * live_float).astype(jnp.bfloat16))
    key_positions = (page_offsets[:, None] + in_page[None, :]).reshape(-1)
    key_live = live_mask.reshape(-1)
    turned_q = rotate(queries.astype(jnp.float32).reshape(QN, H, HD), query_positions)
    turned_q = lax.optimization_barrier(turned_q.astype(jnp.bfloat16))
    per_group = H // KV
    grouped_q = turned_q.reshape(QN, KV, per_group, HD).transpose(1, 2, 0, 3)
    keys_by_head = new_keys.transpose(1, 0, 2)
    values_by_head = new_values.transpose(1, 0, 2)
    allowed = (key_positions[None, :] <= query_positions[:, None]) & key_live[None, :]

    def one_head(operands):
        query_block, key_block, value_block = operands
        scores = jnp.einsum('gqd,kd->gqk', query_block.astype(jnp.float32), key_block.astype(jnp.float32)) * (HD ** -0.5)
        scores = jnp.where(allowed[None], scores, masked_score)
        row_max = jnp.max(scores, axis=-1, keepdims=True)
        weights = jnp.exp(scores - row_max)
        denominator = jnp.sum(weights, axis=-1)
        rounded = lax.optimization_barrier(weights.astype(jnp.bfloat16))
        summed = jnp.einsum('gqk,kd->gqd', rounded.astype(jnp.float32), value_block.astype(jnp.float32))
        return (summed / denominator[..., None]).astype(jnp.bfloat16)

    attended = lax.map(one_head, (grouped_q, keys_by_head, values_by_head))
    mixed = attended.reshape(H, QN, HD).transpose(1, 0, 2).reshape(QN, H * HD)
    output = jnp.dot(mixed, out_weight, preferred_element_type=jnp.float32).astype(jnp.bfloat16)
    return new_keys.reshape(NPAGES * PAGE, KV * HD), new_values.reshape(NPAGES * PAGE, KV * HD), output
```

```python
import functools
import math

import jax
import jax.numpy as jnp
from jax import lax
from jax.experimental import pallas as pl
from jax.experimental.pallas import tpu as pltpu
from jax.sharding import PartitionSpec as P

H = 128
KV = 8
HD = 128
PAGE = 16


rope_theta = 500000.0
scale_factor = 8.0
low_factor = 1.0
high_factor = 4.0
old_context = 8192.0
masked_score = -1e30


def inverse_freq():
    exponent = jnp.arange(0, HD, 2).astype(jnp.float32) / HD
    base_freq = 1.0 / rope_theta**exponent
    wavelength = 2.0 * math.pi / base_freq
    smooth = (old_context / wavelength - low_factor) / (high_factor - low_factor)
    blended = (1.0 - smooth) * base_freq / scale_factor + smooth * base_freq
    short_wave = wavelength < old_context / high_factor
    longer = wavelength > old_context / low_factor
    return jnp.where(short_wave, base_freq, jnp.where(longer, base_freq / scale_factor, blended))


def rotate(values, positions):
    angle = positions.astype(jnp.float32)[:, None] * inverse_freq()[None, :]
    cosine = jnp.cos(angle)[:, None, :]
    sine_part = jnp.sin(angle)[:, None, :]
    half_size = values.shape[-1] // 2
    first_half = values[..., :half_size]
    second = values[..., half_size:]
    return jnp.concatenate(
        [first_half * cosine - second * sine_part, second * cosine + first_half * sine_part],
        axis=-1,
    )


def body(
    pool_keys,
    pool_values,
    key_scales,
    value_scales,
    page_source,
    page_lengths,
    page_offsets,
    query_positions,
    queries,
    out_weight,
):
    devices = lax.axis_size("ctx")
    here_index = lax.axis_index("ctx")
    slot_count = key_scales.shape[0]
    page_count = page_source.shape[0]
    query_count = queries.shape[0]
    local_heads = queries.shape[1] // HD
    per_group = H // KV
    in_page = jnp.arange(PAGE, dtype=jnp.int32)
    inverse = (
        jnp.zeros((page_count,), jnp.int32)
        .at[page_source]
        .set(jnp.arange(page_count, dtype=jnp.int32))
    )
    held_pages = lax.dynamic_slice_in_dim(inverse, here_index * slot_count, slot_count)
    held_live = in_page[None, :] < page_lengths[held_pages][:, None]
    live_float = held_live.reshape(-1).astype(jnp.float32)[:, None, None]
    scaled_keys = (
        pool_keys.reshape(slot_count, PAGE, KV, HD).astype(jnp.float32)
        * key_scales[:, None, :, None]
    )
    scaled_values = (
        pool_values.reshape(slot_count, PAGE, KV, HD).astype(jnp.float32)
        * value_scales[:, None, :, None]
    )
    turned = rotate(
        scaled_keys.reshape(slot_count * PAGE, KV, HD), jnp.repeat(page_offsets[held_pages], PAGE)
    )
    slot_keys = (turned * live_float).astype(jnp.bfloat16).reshape(slot_count, PAGE * KV * HD)
    slot_values = (
        (scaled_values.reshape(slot_count * PAGE, KV, HD) * live_float)
        .astype(jnp.bfloat16)
        .reshape(slot_count, PAGE * KV * HD)
    )
    owner_device = held_pages // slot_count
    routing = (owner_device[None, :] == jnp.arange(devices, dtype=jnp.int32)[:, None]).astype(
        jnp.bfloat16
    )
    outgoing_keys = jnp.dot(routing, slot_keys, preferred_element_type=jnp.float32).astype(
        jnp.bfloat16
    )
    outgoing_values = jnp.dot(routing, slot_values, preferred_element_type=jnp.float32).astype(
        jnp.bfloat16
    )
    arrived_keys, arrived_values = (
        lax.all_to_all(outgoing_keys, "ctx", split_axis=0, concat_axis=0, tiled=True),
        lax.all_to_all(outgoing_values, "ctx", split_axis=0, concat_axis=0, tiled=True),
    )
    assembled_pages = here_index * slot_count + jnp.arange(slot_count, dtype=jnp.int32)
    sender = page_source[assembled_pages] // slot_count
    picking = (sender[:, None] == jnp.arange(devices, dtype=jnp.int32)[None, :]).astype(
        jnp.bfloat16
    )
    new_keys = jnp.dot(picking, arrived_keys, preferred_element_type=jnp.float32).astype(
        jnp.bfloat16
    ).reshape(slot_count * PAGE, KV * HD)
    new_values = jnp.dot(picking, arrived_values, preferred_element_type=jnp.float32).astype(
        jnp.bfloat16
    ).reshape(slot_count * PAGE, KV * HD)
    local_keys = slot_keys.reshape(slot_count * PAGE, KV * HD)
    local_values = slot_values.reshape(slot_count * PAGE, KV * HD)
    local_tokens = local_keys.shape[0]
    turned_q = rotate(
        queries.astype(jnp.float32).reshape(query_count, local_heads, HD), query_positions
    )
    own_queries = turned_q.astype(jnp.bfloat16).transpose(1, 0, 2)
    keys_by_head = local_keys.reshape(local_tokens, KV, HD).transpose(1, 0, 2)
    values_by_head = local_values.reshape(local_tokens, KV, HD).transpose(1, 0, 2)
    head_keys, head_values = (
        lax.all_to_all(jnp.repeat(keys_by_head, per_group // local_heads, axis=0), "ctx", split_axis=0, concat_axis=0, tiled=True),
        lax.all_to_all(jnp.repeat(values_by_head, per_group // local_heads, axis=0), "ctx", split_axis=0, concat_axis=0, tiled=True),
    )
    key_positions = (page_offsets[inverse][:, None] + in_page[None, :]).reshape(-1)
    key_live = (in_page[None, :] < page_lengths[inverse][:, None]).reshape(-1)
    key_positions, key_live = (key_positions, key_live)
    allowed = (key_positions[None, :] <= query_positions[:, None]) & key_live[None, :]
    span_devices = max(1, min(devices, 4096 // local_tokens))
    while span_devices > 1 and devices % span_devices:
        span_devices -= 1
    block_count = devices // span_devices
    key_blocks = head_keys.reshape(block_count, span_devices * local_tokens, HD)
    value_blocks = head_values.reshape(block_count, span_devices * local_tokens, HD)
    allowed_blocks = allowed.reshape(
        query_count, block_count, span_devices * local_tokens
    ).transpose(1, 0, 2)

    def block_scores(key_block, allow_block):
        scores = jnp.einsum(
            "hqd,kd->hqk", own_queries, key_block, preferred_element_type=jnp.float32
        ) * HD ** (-0.5)
        return jnp.where(allow_block[None], scores, masked_score)

    block_max = lax.map(
        lambda operands: jnp.max(block_scores(operands[0], operands[1]), axis=-1),
        (key_blocks, allowed_blocks),
    )
    row_max = jnp.max(block_max, axis=0)

    def weigh_block(operands):
        key_block, value_block, allow_block = operands
        weights = jnp.exp(block_scores(key_block, allow_block) - row_max[..., None])
        denominator = jnp.sum(weights, axis=-1)
        summed = jnp.einsum(
            "hqk,kd->hqd",
            weights.astype(jnp.bfloat16),
            value_block,
            preferred_element_type=jnp.float32,
        )
        return (summed, denominator)

    summed, denominator = lax.map(weigh_block, (key_blocks, value_blocks, allowed_blocks))
    summed = jnp.sum(summed, axis=0)
    denominator = jnp.sum(denominator, axis=0)
    attended = (summed / denominator[..., None]).astype(jnp.bfloat16)
    mixed = attended.transpose(1, 0, 2).reshape(query_count, local_heads * HD)
    reduced = lax.psum_scatter(
        lax.dot_general(
            out_weight, mixed, (((0,), (1,)), ((), ())), preferred_element_type=jnp.float32
        ),
        "ctx",
        scatter_dimension=0,
        tiled=True,
    )
    output = reduced.T.astype(jnp.bfloat16)
    return (new_keys, new_values, output)


def fused_kernel(
    n,
    source_ref,
    length_ref,
    offset_ref,
    position_ref,
    freq_ref,
    position_row,
    pool_keys,
    pool_values,
    key_scales,
    value_scales,
    queries,
    weight,
    out_keys,
    out_values,
    out,
    wv,
    kbuf,
    vbuf,
    scale_own,
    scale_all,
    scale_rows,
    cos_page,
    sin_page,
    cos_query,
    sin_query,
    turned,
    keys,
    values,
    values_t,
    bias,
    scores,
    attended,
    core_send,
    core_recv,
    kept,
    y_send,
    y_recv,
    z_send,
    z_recv,
    w_sem,
    own_sem,
    a_send,
    a_recv,
    f_send,
    f_recv,
    p_own,
    p_send,
    p_recv,
    c_ssem,
    c_rsem,
    y_ssem,
    y_rsem,
    z_ssem,
    z_rsem,
):
    f32, bf16 = jnp.float32, jnp.bfloat16
    chips = n // 2
    planes = chips // 2
    me = lax.axis_index("ctx")
    core = lax.rem(me, 2)
    chip = me // 2
    y = lax.rem(chip, 2)
    z = chip // 2
    partner = chip * 2 + 1 - core
    tokens = pool_keys.shape[0] * PAGE
    slots = key_scales.shape[0]
    pages = source_ref.shape[0]
    qn = queries.shape[0]
    heads = queries.shape[1] // HD
    width = out.shape[1]
    half = HD // 2

    def wait_weight(d):
        pltpu.make_async_copy(
            weight.at[:, pl.ds(pl.multiple_of(d * width, width), width)], wv.at[d], w_sem.at[d]
        ).wait()

    @pl.loop(0, n)
    def _(d):
        pltpu.make_async_copy(
            weight.at[:, pl.ds(pl.multiple_of(d * width, width), width)], wv.at[d], w_sem.at[d]
        ).start()

    scale_own[...] = jnp.zeros_like(scale_own)
    scale_own[0, :, 0:KV] = key_scales[...]
    scale_own[1, :, 0:KV] = value_scales[...]

    def remote(src, dst, ssem, rsem, to):
        return pltpu.make_async_remote_copy(
            src_ref=src, dst_ref=dst, send_sem=ssem, recv_sem=rsem, device_id={"ctx": to}
        )

    barrier = pltpu.get_barrier_semaphore()

    @pl.loop(1, chips)
    def _(s):
        pl.semaphore_signal(
            barrier, inc=1, device_id={"ctx": lax.rem(chip + s, chips) * 2 + core}
        )

    pl.semaphore_signal(barrier, inc=1, device_id={"ctx": partner})
    pl.semaphore_wait(barrier, chips)

    def rows_of(ref, device):
        return ref.at[pl.ds(pl.multiple_of(device * tokens, tokens), tokens), :]

    def head_of(ref, head):
        return ref.at[:, pl.ds(pl.multiple_of(head * HD, HD), HD)]

    def pool_head(ref, head):
        return ref.at[:, :, pl.ds(pl.multiple_of(head * HD, HD), HD)]

    def pages_of(ref, device):
        return ref.at[pl.ds(device * slots, slots)]

    def first_hop(s):
        to = lax.rem(chip + s, chips)
        dev = to * 2 + core
        return (
            remote(pool_head(pool_keys, to), pages_of(kbuf, me), a_send.at[0, to], a_recv.at[0, chip], dev),
            remote(pool_head(pool_values, to), pages_of(vbuf, me), a_send.at[1, to], a_recv.at[1, chip], dev),
            remote(scale_own, scale_all.at[:, me], a_send.at[2, to], a_recv.at[2, chip], dev),
        )

    def arrivals(s):
        frm = lax.rem(chip + s, chips)
        dev = frm * 2 + core
        return (
            remote(pages_of(kbuf, dev), pages_of(kbuf, dev), a_send.at[0, frm], a_recv.at[0, frm], dev),
            remote(pages_of(vbuf, dev), pages_of(vbuf, dev), a_send.at[1, frm], a_recv.at[1, frm], dev),
            remote(scale_own, scale_all.at[:, dev], a_send.at[2, frm], a_recv.at[2, frm], dev),
        )

    def forward(frm, block_core):
        dev = frm * 2 + block_core
        return (
            remote(pages_of(kbuf, dev), pages_of(kbuf, dev), f_send.at[0, frm], f_recv.at[0, frm], partner),
            remote(pages_of(vbuf, dev), pages_of(vbuf, dev), f_send.at[1, frm], f_recv.at[1, frm], partner),
            remote(scale_all.at[:, dev], scale_all.at[:, dev], f_send.at[2, frm], f_recv.at[2, frm], partner),
        )

    @pl.loop(1, chips)
    def _(s):
        for copy in first_hop(s):
            copy.start()

    own = (
        pltpu.make_async_copy(pool_head(pool_keys, chip), pages_of(kbuf, me), own_sem.at[0]),
        pltpu.make_async_copy(pool_head(pool_values, chip), pages_of(vbuf, me), own_sem.at[1]),
        pltpu.make_async_copy(scale_own, scale_all.at[:, me], own_sem.at[2]),
    )
    for copy in own:
        copy.start()

    freq = freq_ref[...]

    @pl.loop(0, pages, unroll=8)
    def _(c):
        cos_page[pl.ds(c, 1), :] = freq * offset_ref[c].astype(f32)

    @pl.loop(0, qn, unroll=8)
    def _(c):
        cos_query[pl.ds(c, 1), :] = freq * position_ref[c].astype(f32)

    def angles(cos_ref, sin_ref):
        angle = cos_ref[...]
        lane = lax.broadcasted_iota(jnp.int32, angle.shape, 1)
        sine = jnp.sin(angle)
        sin_ref[...] = jnp.where(lane < half, -sine, sine)
        cos_ref[...] = jnp.cos(angle)

    for copy in own:
        copy.wait()
    for copy in forward(chip, core):
        copy.start()
    angles(cos_page, sin_page)
    angles(cos_query, sin_query)

    cosine, sine = cos_query[...], sin_query[...]
    for h in range(heads):
        x = queries[:, h * HD : (h + 1) * HD].astype(f32)
        turned[h * qn : (h + 1) * qn, :] = (x * cosine + pltpu.roll(x, half, 1) * sine).astype(bf16)

    @pl.loop(1, chips)
    def _(s):
        frm = lax.rem(chip + s, chips)
        for copy, onward in zip(arrivals(s), forward(frm, core)):
            copy.wait_recv()
            onward.start()

    @pl.loop(0, chips)
    def _(frm):
        for copy in forward(frm, 1 - core):
            copy.wait_recv()

    head_lane = lax.broadcasted_iota(jnp.int32, (n * slots, HD), 1) == chip
    for kind in range(2):
        block = scale_all[kind].reshape(n * slots, HD)
        picked = jnp.sum(jnp.where(head_lane, block, 0.0), axis=1, keepdims=True)
        scale_rows[kind] = jnp.broadcast_to(picked, (n * slots, HD))

    row = lax.broadcasted_iota(jnp.int32, (PAGE, HD), 0)
    q_row = position_row[...]

    @pl.loop(0, pages, unroll=4)
    def _(c):
        s = source_ref[c]
        live = row < length_ref[c]
        where_to = pl.ds(pl.multiple_of(c * PAGE, PAGE), PAGE)
        k = kbuf[s].astype(f32) * scale_rows[0, pl.ds(s, 1), :]
        k = k * cos_page[pl.ds(c, 1), :] + pltpu.roll(k, half, 1) * sin_page[pl.ds(c, 1), :]
        keys[where_to, :] = jnp.where(live, k, 0.0).astype(bf16)
        v = vbuf[s].astype(f32) * scale_rows[1, pl.ds(s, 1), :]
        values[where_to, :] = jnp.where(live, v, 0.0).astype(bf16)
        allowed = jnp.logical_and(live, row + offset_ref[c] <= q_row)
        bias[where_to, :] = jnp.where(allowed, 0.0, masked_score)

    def pages_out(s):
        to = lax.rem(chip + s, chips)
        dev = to * 2 + core
        return (
            remote(rows_of(keys, dev), head_of(out_keys, chip), p_send.at[0, to], p_recv.at[0, chip], dev),
            remote(rows_of(values, dev), head_of(out_values, chip), p_send.at[1, to], p_recv.at[1, chip], dev),
        )

    def pages_in(s):
        frm = lax.rem(chip + s, chips)
        dev = frm * 2 + core
        return (
            remote(rows_of(keys, me), head_of(out_keys, frm), p_send.at[0, frm], p_recv.at[0, frm], dev),
            remote(rows_of(values, me), head_of(out_values, frm), p_send.at[1, frm], p_recv.at[1, frm], dev),
        )

    @pl.loop(1, chips)
    def _(s):
        for copy in pages_out(s):
            copy.start()

    own_pages = (
        pltpu.make_async_copy(rows_of(keys, me), head_of(out_keys, chip), p_own.at[0]),
        pltpu.make_async_copy(rows_of(values, me), head_of(out_values, chip), p_own.at[1]),
    )
    for copy in own_pages:
        copy.start()

    total = keys.shape[0]
    block = 256
    for at in range(0, total, block):
        values_t[:, at : at + block] = values[at : at + block, :].astype(f32).T.astype(bf16)
    span = 2 * qn
    scale = HD ** (-0.5)

    @pl.loop(0, heads // 2)
    def _(pair):
        q2 = turned[pl.ds(pl.multiple_of(pair * span, span), span), :]

        def score_block(b, peak):
            at = pl.ds(pl.multiple_of(b * block, block), block)
            s = lax.dot_general(
                keys[at, :], q2, (((1,), (1,)), ((), ())), preferred_element_type=f32
            )
            mask = bias[at, :]
            s = s * scale + jnp.concatenate([mask, mask], axis=1)
            scores[at, :] = s
            return jnp.maximum(peak, jnp.max(s, axis=0, keepdims=True))

        peak = lax.fori_loop(
            0, total // block, score_block, jnp.full((1, span), masked_score, f32), unroll=2
        )

        def weigh(b, carry):
            denominator, summed = carry
            start = pl.multiple_of(b * block, block)
            p = jnp.exp(scores[pl.ds(start, block), :] - peak)
            denominator = denominator + jnp.sum(p, axis=0, keepdims=True)
            summed = summed + jnp.dot(
                values_t[:, pl.ds(start, block)], p.astype(bf16), preferred_element_type=f32
            )
            return denominator, summed

        denominator, summed = lax.fori_loop(
            0,
            total // block,
            weigh,
            (jnp.zeros((1, span), f32), jnp.zeros((HD, span), f32)),
            unroll=2,
        )
        mixed = summed / denominator
        for j in range(2):
            attended[:, pl.ds(pl.multiple_of((2 * pair + j) * HD, HD), HD)] = (
                mixed[:, j * qn : (j + 1) * qn].T.astype(bf16)
            )

    piece = min(width, 256)

    def project(d, store):
        wait_weight(d)

        @pl.loop(0, width, step=piece)
        def _(at):
            cols = pl.ds(pl.multiple_of(at, piece), piece)
            store(
                cols,
                jnp.dot(attended[...], wv[d, :, cols], preferred_element_type=f32),
            )

    def across_core(t):
        return remote(core_send.at[t], core_recv.at[t], c_ssem.at[t], c_rsem.at[t], partner)

    def across_y(s):
        dev = (z * 2 + 1 - y) * 2 + core
        return remote(y_send.at[s], y_recv.at[s], y_ssem.at[s], y_rsem.at[s], dev)

    def across_z(s):
        dev = (lax.rem(z + 1 + s, planes) * 2 + y) * 2 + core
        return remote(z_send.at[s], z_recv.at[s], z_ssem.at[s], z_rsem.at[s], dev)

    def chip_sum(s, other):
        t = 2 * s + (0 if other else 1)
        q = lax.rem(z + 1 + s, planes) * 2 + (1 - y if other else y)

        def to_partner(cols, x):
            core_send[t, :, cols] = x.astype(bf16)

        project(q * 2 + 1 - core, to_partner)
        across_core(t).start()

        def keep(cols, x):
            kept[s, :, cols] = x

        project(q * 2 + core, keep)
        across_core(t).wait_recv()

    @pl.loop(0, planes)
    def _(s):
        chip_sum(s, True)
        y_send[s] = (kept[s] + core_recv[2 * s].astype(f32)).astype(bf16)
        across_y(s).start()

    @pl.loop(0, planes)
    def _(s):
        chip_sum(s, False)
        kept[s] = kept[s] + core_recv[2 * s + 1].astype(f32)

    @pl.loop(0, planes - 1)
    def _(s):
        across_y(s).wait_recv()
        z_send[s] = (kept[s] + y_recv[s].astype(f32)).astype(bf16)
        across_z(s).start()

    across_y(planes - 1).wait_recv()
    kept[planes - 1] = kept[planes - 1] + y_recv[planes - 1].astype(f32)

    @pl.loop(0, planes - 1)
    def _(s):
        across_z(s).wait_recv()
        kept[planes - 1] = kept[planes - 1] + z_recv[s].astype(f32)

    out[...] = kept[planes - 1].astype(bf16)

    for copy in own_pages:
        copy.wait()

    @pl.loop(1, chips)
    def _(s):
        for copy in pages_in(s):
            copy.wait_recv()
        for copy in pages_out(s):
            copy.wait_send()
        for copy in first_hop(s):
            copy.wait_send()

    @pl.loop(0, chips)
    def _(frm):
        for copy in forward(frm, core):
            copy.wait_send()

    @pl.loop(0, planes)
    def _(s):
        across_core(2 * s).wait_send()
        across_core(2 * s + 1).wait_send()
        across_y(s).wait_send()

    @pl.loop(0, planes - 1)
    def _(s):
        across_z(s).wait_send()


def fused_body(
    pool_keys,
    pool_values,
    key_scales,
    value_scales,
    page_source,
    page_lengths,
    page_offsets,
    query_positions,
    queries,
    out_weight,
):
    n = lax.axis_size("ctx")
    chips = n // 2
    planes = chips // 2
    tokens, features = pool_keys.shape
    total = n * tokens
    slots = key_scales.shape[0]
    pages = page_source.shape[0]
    qn = queries.shape[0]
    heads = queries.shape[1] // HD
    rows, columns = out_weight.shape
    width = columns // n
    f32, bf16 = jnp.float32, jnp.bfloat16
    freq = jnp.tile(inverse_freq()[None, :], (1, 2))
    smem = pl.BlockSpec(memory_space=pltpu.SMEM)
    vmem = pl.BlockSpec(memory_space=pltpu.VMEM)
    hbm = pl.BlockSpec(memory_space=pl.ANY)
    dma = pltpu.SemaphoreType.DMA
    return pl.pallas_call(
        functools.partial(fused_kernel, n),
        out_shape=(
            jax.ShapeDtypeStruct((tokens, features), bf16),
            jax.ShapeDtypeStruct((tokens, features), bf16),
            jax.ShapeDtypeStruct((qn, width), bf16),
        ),
        in_specs=[smem] * 4 + [vmem, vmem, hbm, hbm, vmem, vmem, vmem, hbm],
        out_specs=(hbm, hbm, vmem),
        scratch_shapes=[
            pltpu.VMEM((n, rows, width), bf16),
            pltpu.VMEM((pages, PAGE, HD), bf16),
            pltpu.VMEM((pages, PAGE, HD), bf16),
            pltpu.VMEM((2, slots, HD), f32),
            pltpu.VMEM((2, n, slots, HD), f32),
            pltpu.VMEM((2, n * slots, HD), f32),
            pltpu.VMEM((pages, HD), f32),
            pltpu.VMEM((pages, HD), f32),
            pltpu.VMEM((qn, HD), f32),
            pltpu.VMEM((qn, HD), f32),
            pltpu.VMEM((heads * qn, HD), bf16),
            pltpu.VMEM((total, HD), bf16),
            pltpu.VMEM((total, HD), bf16),
            pltpu.VMEM((HD, total), bf16),
            pltpu.VMEM((total, qn), f32),
            pltpu.VMEM((total, 2 * qn), f32),
            pltpu.VMEM((qn, heads * HD), bf16),
            pltpu.VMEM((chips, qn, width), bf16),
            pltpu.VMEM((chips, qn, width), bf16),
            pltpu.VMEM((planes, qn, width), f32),
            pltpu.VMEM((planes, qn, width), bf16),
            pltpu.VMEM((planes, qn, width), bf16),
            pltpu.VMEM((planes - 1, qn, width), bf16),
            pltpu.VMEM((planes - 1, qn, width), bf16),
            dma((n,)),
            dma((3,)),
            dma((3, chips)),
            dma((3, chips)),
            dma((3, chips)),
            dma((3, chips)),
            dma((2,)),
            dma((2, chips)),
            dma((2, chips)),
            dma((chips,)),
            dma((chips,)),
            dma((planes,)),
            dma((planes,)),
            dma((planes - 1,)),
            dma((planes - 1,)),
        ],
        compiler_params=pltpu.CompilerParams(
            collective_id=0, has_side_effects=True, vmem_limit_bytes=60 * 2**20
        ),
    )(
        page_source,
        page_lengths,
        page_offsets,
        query_positions,
        freq,
        query_positions.reshape(1, qn),
        pool_keys.reshape(slots, PAGE, features),
        pool_values.reshape(slots, PAGE, features),
        key_scales,
        value_scales,
        queries,
        out_weight,
    )


def solution(mesh):
    in_specs = (
        P(("groups", "ctx"), None),
        P(("groups", "ctx"), None),
        P(("groups", "ctx"), None),
        P(("groups", "ctx"), None),
        P("groups"),
        P("groups"),
        P("groups"),
        P("groups"),
        P("groups", "ctx"),
        P("ctx", None),
    )
    out_specs = (P(("groups", "ctx"), None), P(("groups", "ctx"), None), P("groups", "ctx"))
    chosen = fused_body if mesh.shape["ctx"] == 2 * KV else body
    return jax.shard_map(chosen, mesh=mesh, in_specs=in_specs, out_specs=out_specs, check_vma=False)
```

```python
import functools
import math

import jax
import jax.numpy as jnp
from jax import lax
from jax.experimental import pallas as pl
from jax.experimental.pallas import tpu as pltpu
from jax.sharding import PartitionSpec as P

H = 128
KV = 8
HD = 128
PAGE = 16


rope_theta = 500000.0
scale_factor = 8.0
low_factor = 1.0
high_factor = 4.0
old_context = 8192.0
masked_score = -1e30


def inverse_freq():
    exponent = jnp.arange(0, HD, 2).astype(jnp.float32) / HD
    base_freq = 1.0 / rope_theta**exponent
    wavelength = 2.0 * math.pi / base_freq
    smooth = (old_context / wavelength - low_factor) / (high_factor - low_factor)
    blended = (1.0 - smooth) * base_freq / scale_factor + smooth * base_freq
    short_wave = wavelength < old_context / high_factor
    longer = wavelength > old_context / low_factor
    return jnp.where(short_wave, base_freq, jnp.where(longer, base_freq / scale_factor, blended))


def rotate(values, positions):
    angle = positions.astype(jnp.float32)[:, None] * inverse_freq()[None, :]
    cosine = jnp.cos(angle)[:, None, :]
    sine_part = jnp.sin(angle)[:, None, :]
    half_size = values.shape[-1] // 2
    first_half = values[..., :half_size]
    second = values[..., half_size:]
    return jnp.concatenate(
        [first_half * cosine - second * sine_part, second * cosine + first_half * sine_part],
        axis=-1,
    )


def body(
    pool_keys,
    pool_values,
    key_scales,
    value_scales,
    page_source,
    page_lengths,
    page_offsets,
    query_positions,
    queries,
    out_weight,
):
    devices = lax.axis_size("ctx")
    here_index = lax.axis_index("ctx")
    slot_count = key_scales.shape[0]
    page_count = page_source.shape[0]
    query_count = queries.shape[0]
    local_heads = queries.shape[1] // HD
    per_group = H // KV
    in_page = jnp.arange(PAGE, dtype=jnp.int32)
    inverse = (
        jnp.zeros((page_count,), jnp.int32)
        .at[page_source]
        .set(jnp.arange(page_count, dtype=jnp.int32))
    )
    held_pages = lax.dynamic_slice_in_dim(inverse, here_index * slot_count, slot_count)
    held_live = in_page[None, :] < page_lengths[held_pages][:, None]
    live_float = held_live.reshape(-1).astype(jnp.float32)[:, None, None]
    scaled_keys = (
        pool_keys.reshape(slot_count, PAGE, KV, HD).astype(jnp.float32)
        * key_scales[:, None, :, None]
    )
    scaled_values = (
        pool_values.reshape(slot_count, PAGE, KV, HD).astype(jnp.float32)
        * value_scales[:, None, :, None]
    )
    turned = rotate(
        scaled_keys.reshape(slot_count * PAGE, KV, HD), jnp.repeat(page_offsets[held_pages], PAGE)
    )
    slot_keys = (turned * live_float).astype(jnp.bfloat16).reshape(slot_count, PAGE * KV * HD)
    slot_values = (
        (scaled_values.reshape(slot_count * PAGE, KV, HD) * live_float)
        .astype(jnp.bfloat16)
        .reshape(slot_count, PAGE * KV * HD)
    )
    owner_device = held_pages // slot_count
    routing = (owner_device[None, :] == jnp.arange(devices, dtype=jnp.int32)[:, None]).astype(
        jnp.bfloat16
    )
    outgoing_keys = jnp.dot(routing, slot_keys, preferred_element_type=jnp.float32).astype(
        jnp.bfloat16
    )
    outgoing_values = jnp.dot(routing, slot_values, preferred_element_type=jnp.float32).astype(
        jnp.bfloat16
    )
    arrived_keys, arrived_values = (
        lax.all_to_all(outgoing_keys, "ctx", split_axis=0, concat_axis=0, tiled=True),
        lax.all_to_all(outgoing_values, "ctx", split_axis=0, concat_axis=0, tiled=True),
    )
    assembled_pages = here_index * slot_count + jnp.arange(slot_count, dtype=jnp.int32)
    sender = page_source[assembled_pages] // slot_count
    picking = (sender[:, None] == jnp.arange(devices, dtype=jnp.int32)[None, :]).astype(
        jnp.bfloat16
    )
    new_keys = jnp.dot(picking, arrived_keys, preferred_element_type=jnp.float32).astype(
        jnp.bfloat16
    ).reshape(slot_count * PAGE, KV * HD)
    new_values = jnp.dot(picking, arrived_values, preferred_element_type=jnp.float32).astype(
        jnp.bfloat16
    ).reshape(slot_count * PAGE, KV * HD)
    local_keys = slot_keys.reshape(slot_count * PAGE, KV * HD)
    local_values = slot_values.reshape(slot_count * PAGE, KV * HD)
    local_tokens = local_keys.shape[0]
    turned_q = rotate(
        queries.astype(jnp.float32).reshape(query_count, local_heads, HD), query_positions
    )
    own_queries = turned_q.astype(jnp.bfloat16).transpose(1, 0, 2)
    keys_by_head = local_keys.reshape(local_tokens, KV, HD).transpose(1, 0, 2)
    values_by_head = local_values.reshape(local_tokens, KV, HD).transpose(1, 0, 2)
    head_keys, head_values = (
        lax.all_to_all(jnp.repeat(keys_by_head, per_group // local_heads, axis=0), "ctx", split_axis=0, concat_axis=0, tiled=True),
        lax.all_to_all(jnp.repeat(values_by_head, per_group // local_heads, axis=0), "ctx", split_axis=0, concat_axis=0, tiled=True),
    )
    key_positions = (page_offsets[inverse][:, None] + in_page[None, :]).reshape(-1)
    key_live = (in_page[None, :] < page_lengths[inverse][:, None]).reshape(-1)
    key_positions, key_live = (key_positions, key_live)
    allowed = (key_positions[None, :] <= query_positions[:, None]) & key_live[None, :]
    span_devices = max(1, min(devices, 4096 // local_tokens))
    while span_devices > 1 and devices % span_devices:
        span_devices -= 1
    block_count = devices // span_devices
    key_blocks = head_keys.reshape(block_count, span_devices * local_tokens, HD)
    value_blocks = head_values.reshape(block_count, span_devices * local_tokens, HD)
    allowed_blocks = allowed.reshape(
        query_count, block_count, span_devices * local_tokens
    ).transpose(1, 0, 2)

    def block_scores(key_block, allow_block):
        scores = jnp.einsum(
            "hqd,kd->hqk", own_queries, key_block, preferred_element_type=jnp.float32
        ) * HD ** (-0.5)
        return jnp.where(allow_block[None], scores, masked_score)

    block_max = lax.map(
        lambda operands: jnp.max(block_scores(operands[0], operands[1]), axis=-1),
        (key_blocks, allowed_blocks),
    )
    row_max = jnp.max(block_max, axis=0)

    def weigh_block(operands):
        key_block, value_block, allow_block = operands
        weights = jnp.exp(block_scores(key_block, allow_block) - row_max[..., None])
        denominator = jnp.sum(weights, axis=-1)
        summed = jnp.einsum(
            "hqk,kd->hqd",
            weights.astype(jnp.bfloat16),
            value_block,
            preferred_element_type=jnp.float32,
        )
        return (summed, denominator)

    summed, denominator = lax.map(weigh_block, (key_blocks, value_blocks, allowed_blocks))
    summed = jnp.sum(summed, axis=0)
    denominator = jnp.sum(denominator, axis=0)
    attended = (summed / denominator[..., None]).astype(jnp.bfloat16)
    mixed = attended.transpose(1, 0, 2).reshape(query_count, local_heads * HD)
    reduced = lax.psum_scatter(
        lax.dot_general(
            out_weight, mixed, (((0,), (1,)), ((), ())), preferred_element_type=jnp.float32
        ),
        "ctx",
        scatter_dimension=0,
        tiled=True,
    )
    output = reduced.T.astype(jnp.bfloat16)
    return (new_keys, new_values, output)


PIECE = 1024


def fused_kernel(
    n,
    source_ref,
    length_ref,
    offset_ref,
    position_ref,
    freq_ref,
    position_row,
    pool_keys,
    pool_values,
    key_scales,
    value_scales,
    queries,
    weight,
    out_keys,
    out_values,
    out,
    wv,
    kbuf,
    vbuf,
    scale_own,
    scale_all,
    scale_rows,
    cos_page,
    sin_page,
    cos_query,
    sin_query,
    turned,
    keys,
    values,
    values_t,
    bias,
    scores,
    attended,
    core_send,
    core_recv,
    kept,
    y_send,
    y_recv,
    z_send,
    z_recv,
    w_sem,
    own_sem,
    a_send,
    a_recv,
    f_send,
    f_recv,
    p_own,
    p_send,
    p_recv,
    c_ssem,
    c_rsem,
    y_ssem,
    y_rsem,
    z_ssem,
    z_rsem,
):
    f32, bf16 = jnp.float32, jnp.bfloat16
    chips = n // 2
    planes = chips // 2
    me = lax.axis_index("ctx")
    core = lax.rem(me, 2)
    chip = me // 2
    y = lax.rem(chip, 2)
    z = chip // 2
    partner = chip * 2 + 1 - core
    tokens = pool_keys.shape[0] * PAGE
    slots = key_scales.shape[0]
    pages = source_ref.shape[0]
    qn = queries.shape[0]
    heads = queries.shape[1] // HD
    width = out.shape[1]
    half = HD // 2

    def wait_weight(d):
        pltpu.make_async_copy(
            weight.at[:, pl.ds(pl.multiple_of(d * width, width), width)], wv.at[d], w_sem.at[d]
        ).wait()

    @pl.loop(0, n)
    def _(d):
        pltpu.make_async_copy(
            weight.at[:, pl.ds(pl.multiple_of(d * width, width), width)], wv.at[d], w_sem.at[d]
        ).start()

    scale_own[...] = jnp.zeros_like(scale_own)
    scale_own[0, :, 0:KV] = key_scales[...]
    scale_own[1, :, 0:KV] = value_scales[...]

    def remote(src, dst, ssem, rsem, to):
        return pltpu.make_async_remote_copy(
            src_ref=src, dst_ref=dst, send_sem=ssem, recv_sem=rsem, device_id={"ctx": to}
        )

    barrier = pltpu.get_barrier_semaphore()

    @pl.loop(1, chips)
    def _(s):
        pl.semaphore_signal(
            barrier, inc=1, device_id={"ctx": lax.rem(chip + s, chips) * 2 + core}
        )

    pl.semaphore_signal(barrier, inc=1, device_id={"ctx": partner})
    pl.semaphore_wait(barrier, chips)

    def rows_of(ref, device):
        return ref.at[pl.ds(pl.multiple_of(device * tokens, tokens), tokens), :]

    def head_of(ref, head):
        return ref.at[:, pl.ds(pl.multiple_of(head * HD, HD), HD)]

    def pool_head(ref, head):
        return ref.at[:, :, pl.ds(pl.multiple_of(head * HD, HD), HD)]

    def pages_of(ref, device):
        return ref.at[pl.ds(device * slots, slots)]

    def first_hop(s):
        to = lax.rem(chip + s, chips)
        dev = to * 2 + core
        return (
            remote(pool_head(pool_keys, to), pages_of(kbuf, me), a_send.at[0, to], a_recv.at[0, chip], dev),
            remote(pool_head(pool_values, to), pages_of(vbuf, me), a_send.at[1, to], a_recv.at[1, chip], dev),
            remote(scale_own, scale_all.at[:, me], a_send.at[2, to], a_recv.at[2, chip], dev),
        )

    def arrivals(s):
        frm = lax.rem(chip + s, chips)
        dev = frm * 2 + core
        return (
            remote(pages_of(kbuf, dev), pages_of(kbuf, dev), a_send.at[0, frm], a_recv.at[0, frm], dev),
            remote(pages_of(vbuf, dev), pages_of(vbuf, dev), a_send.at[1, frm], a_recv.at[1, frm], dev),
            remote(scale_own, scale_all.at[:, dev], a_send.at[2, frm], a_recv.at[2, frm], dev),
        )

    def forward(frm, block_core):
        dev = frm * 2 + block_core
        return (
            remote(pages_of(kbuf, dev), pages_of(kbuf, dev), f_send.at[0, frm], f_recv.at[0, frm], partner),
            remote(pages_of(vbuf, dev), pages_of(vbuf, dev), f_send.at[1, frm], f_recv.at[1, frm], partner),
            remote(scale_all.at[:, dev], scale_all.at[:, dev], f_send.at[2, frm], f_recv.at[2, frm], partner),
        )

    @pl.loop(1, chips)
    def _(s):
        for copy in first_hop(s):
            copy.start()

    own = (
        pltpu.make_async_copy(pool_head(pool_keys, chip), pages_of(kbuf, me), own_sem.at[0]),
        pltpu.make_async_copy(pool_head(pool_values, chip), pages_of(vbuf, me), own_sem.at[1]),
        pltpu.make_async_copy(scale_own, scale_all.at[:, me], own_sem.at[2]),
    )
    for copy in own:
        copy.start()

    freq = freq_ref[...]

    @pl.loop(0, pages, unroll=8)
    def _(c):
        cos_page[pl.ds(c, 1), :] = freq * offset_ref[c].astype(f32)

    @pl.loop(0, qn, unroll=8)
    def _(c):
        cos_query[pl.ds(c, 1), :] = freq * position_ref[c].astype(f32)

    def angles(cos_ref, sin_ref):
        angle = cos_ref[...]
        lane = lax.broadcasted_iota(jnp.int32, angle.shape, 1)
        sine = jnp.sin(angle)
        sin_ref[...] = jnp.where(lane < half, -sine, sine)
        cos_ref[...] = jnp.cos(angle)

    for copy in own:
        copy.wait()
    for copy in forward(chip, core):
        copy.start()
    angles(cos_page, sin_page)
    angles(cos_query, sin_query)

    cosine, sine = cos_query[...], sin_query[...]
    for h in range(heads):
        x = queries[:, h * HD : (h + 1) * HD].astype(f32)
        turned[h * qn : (h + 1) * qn, :] = (x * cosine + pltpu.roll(x, half, 1) * sine).astype(bf16)

    @pl.loop(1, chips)
    def _(s):
        frm = lax.rem(chip + s, chips)
        for copy, onward in zip(arrivals(s), forward(frm, core)):
            copy.wait_recv()
            onward.start()

    @pl.loop(0, chips)
    def _(frm):
        for copy in forward(frm, 1 - core):
            copy.wait_recv()

    head_lane = lax.broadcasted_iota(jnp.int32, (n * slots, HD), 1) == chip
    for kind in range(2):
        block = scale_all[kind].reshape(n * slots, HD)
        picked = jnp.sum(jnp.where(head_lane, block, 0.0), axis=1, keepdims=True)
        scale_rows[kind] = jnp.broadcast_to(picked, (n * slots, HD))

    row = lax.broadcasted_iota(jnp.int32, (PAGE, HD), 0)
    q_row = position_row[...]

    @pl.loop(0, pages, unroll=4)
    def _(c):
        s = source_ref[c]
        live = row < length_ref[c]
        where_to = pl.ds(pl.multiple_of(c * PAGE, PAGE), PAGE)
        k = kbuf[s].astype(f32) * scale_rows[0, pl.ds(s, 1), :]
        k = k * cos_page[pl.ds(c, 1), :] + pltpu.roll(k, half, 1) * sin_page[pl.ds(c, 1), :]
        keys[where_to, :] = jnp.where(live, k, 0.0).astype(bf16)
        v = vbuf[s].astype(f32) * scale_rows[1, pl.ds(s, 1), :]
        values[where_to, :] = jnp.where(live, v, 0.0).astype(bf16)
        allowed = jnp.logical_and(live, row + offset_ref[c] <= q_row)
        bias[where_to, :] = jnp.where(allowed, 0.0, masked_score)

    def pages_out(s):
        to = lax.rem(chip + s, chips)
        dev = to * 2 + core
        return (
            remote(rows_of(keys, dev), head_of(out_keys, chip), p_send.at[0, to], p_recv.at[0, chip], dev),
            remote(rows_of(values, dev), head_of(out_values, chip), p_send.at[1, to], p_recv.at[1, chip], dev),
        )

    def pages_in(s):
        frm = lax.rem(chip + s, chips)
        dev = frm * 2 + core
        return (
            remote(rows_of(keys, me), head_of(out_keys, frm), p_send.at[0, frm], p_recv.at[0, frm], dev),
            remote(rows_of(values, me), head_of(out_values, frm), p_send.at[1, frm], p_recv.at[1, frm], dev),
        )

    @pl.loop(1, chips)
    def _(s):
        for copy in pages_out(s):
            copy.start()

    own_pages = (
        pltpu.make_async_copy(rows_of(keys, me), head_of(out_keys, chip), p_own.at[0]),
        pltpu.make_async_copy(rows_of(values, me), head_of(out_values, chip), p_own.at[1]),
    )
    for copy in own_pages:
        copy.start()

    total = keys.shape[0]
    block = 256
    for at in range(0, total, block):
        values_t[:, at : at + block] = values[at : at + block, :].astype(f32).T.astype(bf16)
    span = 2 * qn
    scale = HD ** (-0.5)

    @pl.loop(0, heads // 2)
    def _(pair):
        q2 = turned[pl.ds(pl.multiple_of(pair * span, span), span), :]

        def score_block(b, peak):
            at = pl.ds(pl.multiple_of(b * block, block), block)
            s = lax.dot_general(
                keys[at, :], q2, (((1,), (1,)), ((), ())), preferred_element_type=f32
            )
            mask = bias[at, :]
            s = s * scale + jnp.concatenate([mask, mask], axis=1)
            scores[at, :] = s
            return jnp.maximum(peak, jnp.max(s, axis=0, keepdims=True))

        peak = lax.fori_loop(
            0, total // block, score_block, jnp.full((1, span), masked_score, f32), unroll=2
        )

        def weigh(b, carry):
            denominator, summed = carry
            start = pl.multiple_of(b * block, block)
            p = jnp.exp(scores[pl.ds(start, block), :] - peak)
            denominator = denominator + jnp.sum(p, axis=0, keepdims=True)
            summed = summed + jnp.dot(
                values_t[:, pl.ds(start, block)], p.astype(bf16), preferred_element_type=f32
            )
            return denominator, summed

        denominator, summed = lax.fori_loop(
            0,
            total // block,
            weigh,
            (jnp.zeros((1, span), f32), jnp.zeros((HD, span), f32)),
            unroll=2,
        )
        mixed = summed / denominator
        for j in range(2):
            attended[:, pl.ds(pl.multiple_of((2 * pair + j) * HD, HD), HD)] = (
                mixed[:, j * qn : (j + 1) * qn].T.astype(bf16)
            )

    piece = min(width, PIECE)

    def project(d, store):
        wait_weight(d)

        @pl.loop(0, width, step=piece)
        def _(at):
            cols = pl.ds(pl.multiple_of(at, piece), piece)
            store(
                cols,
                jnp.dot(attended[...], wv[d, :, cols], preferred_element_type=f32),
            )

    def across_core(t):
        return remote(core_send.at[t], core_recv.at[t], c_ssem.at[t], c_rsem.at[t], partner)

    def across_y(s):
        dev = (z * 2 + 1 - y) * 2 + core
        return remote(y_send.at[s], y_recv.at[s], y_ssem.at[s], y_rsem.at[s], dev)

    def across_z(s):
        dev = (lax.rem(z + 1 + s, planes) * 2 + y) * 2 + core
        return remote(z_send.at[s], z_recv.at[s], z_ssem.at[s], z_rsem.at[s], dev)

    def chip_at(k):
        return lax.rem(z + 1 + lax.rem(k, planes), planes) * 2 + lax.rem(1 - y + k // planes, 2)

    def for_partner(k):
        def store(cols, x):
            core_send[k, :, cols] = x.astype(bf16)

        project(chip_at(k) * 2 + 1 - core, store)
        across_core(k).start()

    def for_neighbour(k):
        across_core(k).wait_recv()

        def store(cols, x):
            y_send[k, :, cols] = (x + core_recv[k, :, cols].astype(f32)).astype(bf16)

        project(chip_at(k) * 2 + core, store)
        across_y(k).start()

    def for_column(k):
        across_core(k).wait_recv()

        def store(cols, x):
            kept[k - planes, :, cols] = x + core_recv[k, :, cols].astype(f32)

        project(chip_at(k) * 2 + core, store)

    for_partner(0)

    @pl.loop(0, planes)
    def _(k):
        for_partner(k + 1)
        for_neighbour(k)

    @pl.loop(planes, chips - 1)
    def _(k):
        for_partner(k + 1)
        for_column(k)

    for_column(chips - 1)

    @pl.loop(0, planes - 1)
    def _(s):
        across_y(s).wait_recv()
        z_send[s] = (kept[s] + y_recv[s].astype(f32)).astype(bf16)
        across_z(s).start()

    across_y(planes - 1).wait_recv()
    kept[planes - 1] = kept[planes - 1] + y_recv[planes - 1].astype(f32)

    @pl.loop(0, planes - 1)
    def _(s):
        across_z(s).wait_recv()
        kept[planes - 1] = kept[planes - 1] + z_recv[s].astype(f32)

    out[...] = kept[planes - 1].astype(bf16)

    for copy in own_pages:
        copy.wait()

    @pl.loop(1, chips)
    def _(s):
        for copy in pages_in(s):
            copy.wait_recv()
        for copy in pages_out(s):
            copy.wait_send()
        for copy in first_hop(s):
            copy.wait_send()

    @pl.loop(0, chips)
    def _(frm):
        for copy in forward(frm, core):
            copy.wait_send()

    @pl.loop(0, planes)
    def _(s):
        across_core(s).wait_send()
        across_core(s + planes).wait_send()
        across_y(s).wait_send()

    @pl.loop(0, planes - 1)
    def _(s):
        across_z(s).wait_send()


def hand_over(a, b, c, a_out, b_out, c_out, a_buf, b_buf, c_buf, sem):
    ways = ((a, a_buf, a_out), (b, b_buf, b_out), (c, c_buf, c_out))
    inward = [pltpu.make_async_copy(s, v, sem.at[0, i]) for i, (s, v, _) in enumerate(ways)]
    outward = [pltpu.make_async_copy(v, d, sem.at[1, i]) for i, (_, v, d) in enumerate(ways)]
    for copy in inward:
        copy.start()
    for arrive, leave in zip(inward, outward):
        arrive.wait()
        leave.start()
    for copy in outward:
        copy.wait()


def fused_body(
    pool_keys,
    pool_values,
    key_scales,
    value_scales,
    page_source,
    page_lengths,
    page_offsets,
    query_positions,
    queries,
    out_weight,
):
    n = lax.axis_size("ctx")
    chips = n // 2
    planes = chips // 2
    tokens, features = pool_keys.shape
    total = n * tokens
    slots = key_scales.shape[0]
    pages = page_source.shape[0]
    qn = queries.shape[0]
    heads = queries.shape[1] // HD
    rows, columns = out_weight.shape
    width = columns // n
    f32, bf16 = jnp.float32, jnp.bfloat16
    freq = jnp.tile(inverse_freq()[None, :], (1, 2))
    smem = pl.BlockSpec(memory_space=pltpu.SMEM)
    vmem = pl.BlockSpec(memory_space=pltpu.VMEM)
    hbm = pl.BlockSpec(memory_space=pl.ANY)
    dma = pltpu.SemaphoreType.DMA
    results = pl.pallas_call(
        functools.partial(fused_kernel, n),
        out_shape=(
            jax.ShapeDtypeStruct((tokens, features), bf16),
            jax.ShapeDtypeStruct((tokens, features), bf16),
            jax.ShapeDtypeStruct((qn, width), bf16),
        ),
        in_specs=[smem] * 4 + [vmem, vmem, hbm, hbm, vmem, vmem, vmem, hbm],
        out_specs=(hbm, hbm, vmem),
        scratch_shapes=[
            pltpu.VMEM((n, rows, width), bf16),
            pltpu.VMEM((pages, PAGE, HD), bf16),
            pltpu.VMEM((pages, PAGE, HD), bf16),
            pltpu.VMEM((2, slots, HD), f32),
            pltpu.VMEM((2, n, slots, HD), f32),
            pltpu.VMEM((2, n * slots, HD), f32),
            pltpu.VMEM((pages, HD), f32),
            pltpu.VMEM((pages, HD), f32),
            pltpu.VMEM((qn, HD), f32),
            pltpu.VMEM((qn, HD), f32),
            pltpu.VMEM((heads * qn, HD), bf16),
            pltpu.VMEM((total, HD), bf16),
            pltpu.VMEM((total, HD), bf16),
            pltpu.VMEM((HD, total), bf16),
            pltpu.VMEM((total, qn), f32),
            pltpu.VMEM((total, 2 * qn), f32),
            pltpu.VMEM((qn, heads * HD), bf16),
            pltpu.VMEM((chips, qn, width), bf16),
            pltpu.VMEM((chips, qn, width), bf16),
            pltpu.VMEM((planes, qn, width), f32),
            pltpu.VMEM((planes, qn, width), bf16),
            pltpu.VMEM((planes, qn, width), bf16),
            pltpu.VMEM((planes - 1, qn, width), bf16),
            pltpu.VMEM((planes - 1, qn, width), bf16),
            dma((n,)),
            dma((3,)),
            dma((3, chips)),
            dma((3, chips)),
            dma((3, chips)),
            dma((3, chips)),
            dma((2,)),
            dma((2, chips)),
            dma((2, chips)),
            dma((chips,)),
            dma((chips,)),
            dma((planes,)),
            dma((planes,)),
            dma((planes - 1,)),
            dma((planes - 1,)),
        ],
        compiler_params=pltpu.CompilerParams(
            collective_id=0, has_side_effects=True, vmem_limit_bytes=60 * 2**20
        ),
    )(
        page_source,
        page_lengths,
        page_offsets,
        query_positions,
        freq,
        query_positions.reshape(1, qn),
        pool_keys.reshape(slots, PAGE, features),
        pool_values.reshape(slots, PAGE, features),
        key_scales,
        value_scales,
        queries,
        out_weight,
    )
    return pl.pallas_call(
        hand_over,
        out_shape=tuple(jax.ShapeDtypeStruct(r.shape, r.dtype) for r in results),
        in_specs=[hbm] * 3,
        out_specs=(hbm, hbm, hbm),
        scratch_shapes=[pltpu.VMEM(r.shape, r.dtype) for r in results] + [dma((2, 3))],
    )(*results)


def solution(mesh):
    in_specs = (
        P(("groups", "ctx"), None),
        P(("groups", "ctx"), None),
        P(("groups", "ctx"), None),
        P(("groups", "ctx"), None),
        P("groups"),
        P("groups"),
        P("groups"),
        P("groups"),
        P("groups", "ctx"),
        P("ctx", None),
    )
    out_specs = (P(("groups", "ctx"), None), P(("groups", "ctx"), None), P("groups", "ctx"))
    chosen = fused_body if mesh.shape["ctx"] == 2 * KV else body
    return jax.shard_map(chosen, mesh=mesh, in_specs=in_specs, out_specs=out_specs, check_vma=False)
```
